512 devices in a mesh: rows: 16 (over z), src: 32 (over y, x, core).
Axes of the slice: x: 4, y: 4, z: 16, core: 2. Of those that a mesh axis runs over, the one named last changes fastest.
Arguments:
- right_side: bfloat16 [32, 512, 16384], P('rows', None, 'src'), may hold values from -6 to 6
- diag_inverse: bfloat16 [4, 512, 512], replicated, may hold values from -0.25 to 0.25
- factor_u: bfloat16 [32, 4, 512, 384], P('rows', None, 'src'), may hold values from -0.3125 to 0.3125
- factor_v: bfloat16 [32, 4, 512, 384], P('rows', None, 'src'), may hold values from -0.25 to 0.25
- tile_rank: int32 [32, 4], P('rows'), may hold values from 64 to 384, as said below
- block_order: int32 [32], replicated, may hold values from 0 to 31, each once
Outputs:
- panel_solved_values: bfloat16 [4, 512, 16384], P(None, 'rows', 'src')
- trailing: bfloat16 [32, 512, 16384], P('rows', None, 'src')
The draws below stay inside these ranges and needn't reach their ends.
Inputs may be any that keep to these rules, and one draw needn't show every extreme that they name: `tile_rank`: every value from 64 to 384 may occur; both ends occur in every draw.
All inputs are finite; a program needn't handle non-finite values.
Results may differ from the reference program's by a relative error of at most 0.019.
Values may be sent and summed in bfloat16 or wider, within the bound.
A program may use at most 64 MiB of HBM per device.

```python
import jax
import jax.numpy as jnp
from jax import lax

BS = 512
RMAX = 384
RMIN = 64
PANELS = 4
NBLK = 32
SOURCES = 16384


def draw_tile_rank(key, part):
    key = jax.random.fold_in(key, 7)
    first, second, third = jax.random.split(key, 3)
    total = NBLK * PANELS
    ranks = jax.random.randint(first, (NBLK, PANELS), RMIN, RMAX + 1)
    flat = jnp.arange(total, dtype=jnp.int32).reshape(NBLK, PANELS)
    top = jax.random.randint(second, (), 0, total)
    bottom_rows = (top + 1 + jax.random.randint(third, (), 0, total - 1)) % total
    ranks = jnp.where(flat == top, RMAX, ranks)
    ranks = jnp.where(flat == bottom_rows, RMIN, ranks)
    return ranks.astype(jnp.int32)


def block_levels(own_key, shape, pieces, low, largest):
    gain, own = 1.0, jax.random.fold_in(own_key, 6)
    for position, parts in pieces:
        draws = jnp.exp(jax.random.uniform(jax.random.fold_in(own, position), (parts,), jnp.float32, low / len(pieces), largest / len(pieces)))
        gain = gain * jnp.repeat(draws, shape[position] // parts).reshape([-1 if axis == position else 1 for axis in range(len(shape))])
    return gain


def noise(own_key, dims, deviation, most, shards=(), kind=jnp.bfloat16):
    entries = deviation * jax.random.normal(own_key, dims, jnp.float32)
    if shards:
        entries = entries * block_levels(own_key, dims, shards, -0.22, 0.18)
    return jnp.clip(entries, -most, most).astype(kind)


def setup_inputs(seed: int = 0) -> dict:
    keys = jax.random.split(jax.random.key(seed), 7)
    right_side = noise(keys[0], (NBLK, BS, SOURCES), 1.0, 6.0, ((0, 16), (2, 32)))
    diag_inverse = noise(keys[1], (PANELS, BS, BS), BS ** -0.5, 0.25)
    factor_u = noise(keys[2], (NBLK, PANELS, BS, RMAX), RMAX ** -0.5, 0.3125, ((0, 16), (2, 32)))
    factor_v = noise(keys[3], (NBLK, PANELS, BS, RMAX), BS ** -0.5, 0.25, ((0, 16), (2, 32)))
    tile_rank = draw_tile_rank(jax.random.fold_in(keys[6], 71), 0)
    block_order = jax.random.permutation(keys[5], NBLK).astype(jnp.int32)
    return dict(right_side=right_side, diag_inverse=diag_inverse, factor_u=factor_u, factor_v=factor_v, tile_rank=tile_rank, block_order=block_order)


def reference(right_side, diag_inverse, factor_u, factor_v, tile_rank, block_order):
    resid = right_side.astype(jnp.float32)
    columns = jnp.arange(RMAX, dtype=jnp.int32)
    solved = []
    for k in range(PANELS):
        pick = (block_order == k).astype(jnp.float32)
        current = jnp.sum(pick[:, None, None] * resid, axis=0).astype(jnp.bfloat16)
        block_entry = jnp.dot(diag_inverse[k].astype(jnp.float32), current.astype(jnp.float32),
                        precision=lax.Precision.HIGHEST).astype(jnp.bfloat16)
        solved.append(block_entry)
        live = block_order > k
        keep = (columns[None, :] < tile_rank[:, k][:, None]) & live[:, None]
        block_wide = block_entry.astype(jnp.float32)

        def update(items):
            left_factor, right_factor, mask, rows_now = items
            coupling_term = jnp.dot(right_factor.astype(jnp.float32).T, block_wide, precision=lax.Precision.HIGHEST)
            coupling_term = jnp.where(mask[:, None], coupling_term, 0.0).astype(jnp.bfloat16)
            return rows_now - jnp.dot(left_factor.astype(jnp.float32), coupling_term.astype(jnp.float32),
                                      precision=lax.Precision.HIGHEST)

        resid = lax.map(update, (factor_u[:, k], factor_v[:, k], keep, resid))
    return jnp.stack(solved), resid.astype(jnp.bfloat16)
```

```python
import functools

import jax
import jax.numpy as jnp
from jax import lax
from jax.experimental import pallas as pl
from jax.experimental.pallas import tpu as pltpu
from jax.sharding import PartitionSpec as P

MESH = pl.DeviceIdType.MESH
PAIRS = ((1, 0), (2, 0), (2, 1), (3, 0), (3, 1), (3, 2))
Z = 16
SUB = 4
RSR, RSL = 8, 7


def remote(src, dst, send, recv, where):
    return pltpu.make_async_remote_copy(
        src_ref=src, dst_ref=dst, send_sem=send, recv_sem=recv, device_id=where, device_id_type=MESH
    )


def kernel(
    order_ref, rank_ref, x_ref, d_ref, u_ref, v_ref,
    psv_ref, out_ref,
    sel, wr, wl, r, g, pt, pts, ptr, ys, cs,
    rs_sr, rs_rr, rs_sl, rs_rl, ag_sr, ag_rr, ag_sl, ag_rl,
    ps_s, ps_r, pa_s, pa_r, g_s, g_r, p_s, p_r,
):
    z = lax.axis_index("rows")
    me = lax.axis_index("src")
    y, x, c = me // 8, (me // 2) % 4, me % 2
    right, left = {"rows": (z + 1) % Z}, {"rows": (z + Z - 1) % Z}

    def plane(yy, xx, cc):
        return {"src": (yy % 4) * 8 + (xx % 4) * 2 + cc}

    xp, xm, yp, ym = plane(y, x + 1, c), plane(y, x + 3, c), plane(y + 1, x, c), plane(y + 3, x, c)
    sib = plane(y, x, 1 - c)

    barrier = pltpu.get_barrier_semaphore()
    for d in range(1, Z):
        pl.semaphore_signal(barrier, inc=1, device_id={"rows": (z + d) % Z}, device_id_type=MESH)
    for where in (xp, xm, yp, ym, sib):
        pl.semaphore_signal(barrier, inc=1, device_id=where, device_id_type=MESH)

    o = [order_ref[2 * z], order_ref[2 * z + 1]]

    def build(h, _):
        rows, cols = pl.ds((h % 4) * 128, 128), pl.ds((h // 4) * 128, 128)
        x0, x1 = x_ref[0, rows, cols], x_ref[1, rows, cols]
        for k in range(4):
            sel[h, k] = jnp.where(o[0] == k, x0, jnp.where(o[1] == k, x1, jnp.zeros_like(x0)))
        return 0

    lax.fori_loop(0, Z, build, 0)
    wr[0] = sel[(z + 8) % Z]
    wl[0] = sel[(z + Z - 7) % Z]

    lanes = lax.broadcasted_iota(jnp.int32, (16, 384), 1)
    vm = []
    for s in range(2):
        for k in range(4):
            n = s * 4 + k
            limit = jnp.where(o[s] > k, rank_ref[s, k], 0)
            masked = jnp.where(lanes < limit, v_ref[s, k].astype(jnp.float32), 0.0).astype(jnp.bfloat16)
            g[n, y, x, c] = u_ref[s, k]
            g[8 + n, y, x, c] = masked
            vm.append(masked)
    for p, (j, k) in enumerate(PAIRS):
        zero = jnp.zeros((16, 384), jnp.bfloat16)
        pts[p] = jnp.where(o[0] == j, u_ref[0, k], jnp.where(o[1] == j, u_ref[1, k], zero))
        pts[6 + p] = jnp.where(o[0] == j, vm[k], jnp.where(o[1] == j, vm[4 + k], zero))

    pl.semaphore_wait(barrier, Z - 1 + 5)

    def ps_copy(p):
        return remote(pts.at[p], ptr.at[z], ps_s.at[p], ps_r.at[z], {"rows": p})

    def ps_start(p, _):
        @pl.when(p != z)
        def _():
            ps_copy(p).start()
        return 0

    def ps_wait_send(p, _):
        @pl.when(p != z)
        def _():
            ps_copy(p).wait_send()
        return 0

    def ps_wait_recv(q, _):
        @pl.when(q != z)
        def _():
            remote(pts.at[0], ptr.at[q], ps_s.at[0], ps_r.at[q], {"rows": q}).wait_recv()
        return 0

    def pa_copy(q):
        piece = pt.at[z, y, x, c]
        return remote(piece, piece, pa_s.at[q], pa_r.at[z], {"rows": q})

    def pa_start(q, _):
        @pl.when(q != z)
        def _():
            pa_copy(q).start()
        return 0

    def pa_wait_send(q, _):
        @pl.when(q != z)
        def _():
            pa_copy(q).wait_send()
        return 0

    def pa_wait_recv(p, _):
        @pl.when(p != z)
        def _():
            piece = pt.at[p, y, x, c]
            remote(piece, piece, pa_s.at[0], pa_r.at[p], {"rows": p}).wait_recv()
        return 0

    class Gather:
        def __init__(self, buf, n, send, recv):
            self.buf, self.n, self.send, self.recv = buf, n, send, recv

        def part(self, i, lo, hi):
            return pl.ds(i * self.n + lo, hi - lo)

        def bundle(self, i, tiles, stage, yy, xx):
            if stage == 0:
                return self.buf.at[tiles, yy % 4, xx % 4, c]
            if i == 0:
                return self.buf.at[tiles, yy % 4, :, c]
            return self.buf.at[tiles, :, xx % 4, c]

        def copies(self, stage, relay):
            n, half, out = self.n, self.n // 2, []
            for i in range(2):
                along_x = (i == 0) == (stage == 0)
                plus, minus = (xp, xm) if along_x else (yp, ym)
                for d in range(2):
                    where = (plus, minus)[d]
                    back = 1 if d == 0 else -1
                    if relay:
                        tiles = self.part(i, 0, half) if d == 0 else self.part(i, half, n)
                        off_out, off_in = -back, -2 * back
                    else:
                        tiles = self.part(i, 0, n)
                        off_out, off_in = 0, -back
                    yo, xo = (y, x + off_out + 4) if along_x else (y + off_out + 4, x)
                    yi, xi = (y, x + off_in + 4) if along_x else (y + off_in + 4, x)
                    src = self.bundle(i, tiles, stage, yo, xo)
                    dst = self.bundle(i, tiles, stage, yi, xi)
                    slot = ((stage * 2 + relay) * 2 + i) * 2 + d
                    out.append((src, dst, slot, where))
            return out

        def start(self, stage, relay):
            for src, _, slot, where in self.copies(stage, relay):
                remote(src, src, self.send.at[slot], self.recv.at[slot], where).start()

        def wait(self, stage, relay):
            for _, dst, slot, where in self.copies(stage, relay):
                remote(dst, dst, self.send.at[slot], self.recv.at[slot], where).wait_recv()

        def wait_sends(self):
            for stage in range(2):
                for relay in range(2):
                    for src, _, slot, where in self.copies(stage, relay):
                        remote(src, src, self.send.at[slot], self.recv.at[slot], where).wait_send()
            self.sibling(c).wait_send()

        def sibling(self, core):
            whole = self.buf.at[:, :, :, core]
            return remote(whole, whole, self.send.at[16], self.recv.at[16], sib)

    own, panel = Gather(g, 8, g_s, g_r), Gather(pt, 6, p_s, p_r)

    def rs_right(t, u):
        return remote(wr.at[t, u], wr.at[t + 1, u], rs_sr.at[t, u], rs_rr.at[t, u], right)

    def rs_left(t, u):
        return remote(wl.at[t, u], wl.at[t + 1, u], rs_sl.at[t, u], rs_rl.at[t, u], left)

    def rs_step(t, _):
        hr, hl = (z + 8 - t + Z) % Z, (z + Z - 7 + t) % Z
        for u in range(SUB):
            rs_right(t - 1, u).wait_recv()
            wr[t, u] = wr[t, u] + sel[hr, u]
            rs_right(t, u).start()

            @pl.when(t < RSL)
            def _():
                rs_left(t - 1, u).wait_recv()
                wl[t, u] = wl[t, u] + sel[hl, u]
                rs_left(t, u).start()
        return 0

    def ag_right(t, u):
        piece = r.at[(z + Z - t) % Z, u]
        return remote(piece, piece, ag_sr.at[t, u], ag_rr.at[t, u], right)

    def ag_left(t, u):
        piece = r.at[(z + t) % Z, u]
        return remote(piece, piece, ag_sl.at[t, u], ag_rl.at[t, u], left)

    def ag_right_in(t, u):
        piece = r.at[(z + Z - t - 1) % Z, u]
        return remote(piece, piece, ag_sr.at[t, u], ag_rr.at[t, u], right)

    def ag_left_in(t, u):
        piece = r.at[(z + t + 1) % Z, u]
        return remote(piece, piece, ag_sl.at[t, u], ag_rl.at[t, u], left)

    def ag_step(t, _):
        for u in range(SUB):
            ag_right_in(t - 1, u).wait_recv()
            ag_right(t, u).start()

            @pl.when(t < RSL)
            def _():
                ag_left_in(t - 1, u).wait_recv()
                ag_left(t, u).start()
        return 0

    for u in range(SUB):
        rs_right(0, u).start()
        rs_left(0, u).start()
    lax.fori_loop(0, 12, ps_start, 0)
    own.start(0, 0)
    lax.fori_loop(1, 3, rs_step, 0)
    own.wait(0, 0)
    own.start(0, 1)
    lax.fori_loop(3, 4, rs_step, 0)

    @pl.when(z < 12)
    def _():
        ptr[z] = pts[z]
        lax.fori_loop(0, Z, ps_wait_recv, 0)
        total = ptr[0]
        for q in range(1, Z):
            total = total + ptr[q]
        pt[z, y, x, c] = total
        lax.fori_loop(0, Z, pa_start, 0)

    own.wait(0, 1)
    own.start(1, 0)
    lax.fori_loop(4, 7, rs_step, 0)
    own.wait(1, 0)
    own.start(1, 1)
    lax.fori_loop(7, 8, rs_step, 0)
    for u in range(SUB):
        rs_right(RSR - 1, u).wait_recv()
        rs_left(RSL - 1, u).wait_recv()
        r[z, u] = sel[z, u] + wr[RSR, u] + wl[RSL, u]
        ag_right(0, u).start()
        ag_left(0, u).start()
    lax.fori_loop(0, 12, pa_wait_recv, 0)
    panel.start(0, 0)
    own.wait(1, 1)
    own.sibling(c).start()
    lax.fori_loop(1, 3, ag_step, 0)
    panel.wait(0, 0)
    panel.start(0, 1)
    lax.fori_loop(3, 4, ag_step, 0)
    panel.wait(0, 1)
    panel.start(1, 0)
    lax.fori_loop(4, 6, ag_step, 0)
    panel.wait(1, 0)
    panel.start(1, 1)
    own.sibling(1 - c).wait_recv()
    lax.fori_loop(6, 7, ag_step, 0)
    panel.wait(1, 1)
    panel.sibling(c).start()
    lax.fori_loop(7, 8, ag_step, 0)
    for u in range(SUB):
        ag_right_in(RSR - 1, u).wait_recv()
        ag_left_in(RSL - 1, u).wait_recv()
    panel.sibling(1 - c).wait_recv()

    def tile(ref, n):
        return ref[n].reshape(512, 384)

    def couple(v, value):
        return lax.dot_general(v, value, (((0,), (0,)), ((), ())), preferred_element_type=jnp.float32).astype(jnp.bfloat16)

    def solve(i, _):
        def block(k):
            return jnp.concatenate(
                [jnp.concatenate([r[(2 * i + a) * 4 + q, k] for q in range(4)], axis=0) for a in range(2)], axis=1
            )

        cols = pl.ds(pl.multiple_of(i * 256, 256), 256)
        for k in range(4):
            current = block(k)
            if k > 0:
                acc = current.astype(jnp.float32)
                for j in range(k):
                    p = PAIRS.index((k, j))
                    term = couple(tile(pt, 6 + p), ys[j])
                    acc = acc - jnp.dot(tile(pt, p), term, preferred_element_type=jnp.float32)
                current = acc.astype(jnp.bfloat16)
            ys[k] = jnp.dot(d_ref[k], current, preferred_element_type=jnp.float32).astype(jnp.bfloat16)
            psv_ref[k, :, cols] = ys[k, pl.ds(pl.multiple_of(z * 32, 32), 32), :]
        for s in range(2):
            acc = x_ref[s, :, cols].astype(jnp.float32)
            for k in range(4):
                term = couple(tile(g, 8 + s * 4 + k), ys[k])
                acc = acc - jnp.dot(tile(g, s * 4 + k), term, preferred_element_type=jnp.float32)
            out_ref[s, :, cols] = acc.astype(jnp.bfloat16)
        return 0

    lax.fori_loop(0, 2, solve, 0)

    def rs_done(t, _):
        for u in range(SUB):
            rs_right(t, u).wait_send()
            ag_right(t, u).wait_send()

            @pl.when(t < RSL)
            def _():
                rs_left(t, u).wait_send()
                ag_left(t, u).wait_send()
        return 0

    lax.fori_loop(0, RSR, rs_done, 0)
    lax.fori_loop(0, 12, ps_wait_send, 0)

    @pl.when(z < 12)
    def _():
        lax.fori_loop(0, Z, pa_wait_send, 0)

    own.wait_sends()
    panel.wait_sends()


def local(right_side, diag_inverse, factor_u, factor_v, tile_rank, block_order):
    vmem = pl.BlockSpec(memory_space=pltpu.VMEM)
    smem = pl.BlockSpec(memory_space=pltpu.SMEM)
    bf16 = jnp.bfloat16
    dma = pltpu.SemaphoreType.DMA
    return pl.pallas_call(
        kernel,
        out_shape=(
            jax.ShapeDtypeStruct((4, 32, 512), bf16),
            jax.ShapeDtypeStruct((2, 512, 512), bf16),
        ),
        in_specs=[smem, smem, vmem, vmem, vmem, vmem],
        out_specs=(vmem, vmem),
        scratch_shapes=[
            pltpu.VMEM((Z, 4, 128, 128), bf16),
            pltpu.VMEM((RSR + 1, 4, 128, 128), bf16),
            pltpu.VMEM((RSL + 1, 4, 128, 128), bf16),
            pltpu.VMEM((Z, 4, 128, 128), bf16),
            pltpu.VMEM((16, 4, 4, 2, 16, 384), bf16),
            pltpu.VMEM((12, 4, 4, 2, 16, 384), bf16),
            pltpu.VMEM((12, 16, 384), bf16),
            pltpu.VMEM((Z, 16, 384), bf16),
            pltpu.VMEM((4, 512, 256), bf16),
            pltpu.VMEM((8, 128), bf16),
            dma((RSR, SUB)), dma((RSR, SUB)), dma((RSL, SUB)), dma((RSL, SUB)),
            dma((RSR, SUB)), dma((RSR, SUB)), dma((RSL, SUB)), dma((RSL, SUB)),
            dma((12,)), dma((Z,)), dma((Z,)), dma((12,)),
            dma((17,)), dma((17,)), dma((17,)), dma((17,)),
        ],
        compiler_params=pltpu.CompilerParams(
            collective_id=0, has_side_effects=True, vmem_limit_bytes=56 * 2**20
        ),
        cost_estimate=pl.CostEstimate(flops=7_000_000_000, bytes_accessed=8_000_000, transcendentals=0),
    )(block_order, tile_rank, right_side, diag_inverse, factor_u, factor_v)


def solution(mesh):
    placed = (
        P("rows", None, "src"),
        P(),
        P("rows", None, "src", None),
        P("rows", None, "src", None),
        P("rows", None),
        P(),
    )
    return jax.shard_map(
        local,
        mesh=mesh,
        in_specs=placed,
        out_specs=(P(None, "rows", "src"), P("rows", None, "src")),
        check_vma=False,
    )
```

```python
import functools

import jax
import jax.numpy as jnp
from jax import lax
from jax.experimental import pallas as pl
from jax.experimental.pallas import tpu as pltpu
from jax.sharding import PartitionSpec as P

MESH = pl.DeviceIdType.MESH
PAIRS = ((1, 0), (2, 0), (2, 1), (3, 0), (3, 1), (3, 2))
Z = 16
SUB = 4
PARTNERS = (1, 2, 3, 4, 8, 12, 13, 14, 15)
RSR, RSL = 8, 7


def remote(src, dst, send, recv, where):
    return pltpu.make_async_remote_copy(
        src_ref=src, dst_ref=dst, send_sem=send, recv_sem=recv, device_id=where, device_id_type=MESH
    )


def kernel(
    order_ref, rank_ref, x_hbm, d_hbm, u_hbm, v_hbm,
    psv_ref, out_ref,
    x_ref, d_ref, u_ref, v_ref, sel, wr, wl, r, g, pt, pts, near, mid, far, ys,
    in_sem, rs_sr, rs_rr, rs_sl, rs_rl, ag_sr, ag_rr, ag_sl, ag_rl,
    n_s, n_r, f_s, f_r, b_s, b_r, a_s, a_r, g_s, g_r, p_s, p_r,
):
    z = lax.axis_index("rows")
    me = lax.axis_index("src")
    y, x, c = me // 8, lax.rem(me // 2, 4), lax.rem(me, 2)
    group, member = z // 4, lax.rem(z, 4)
    right, left = {"rows": lax.rem(z + 1, Z)}, {"rows": lax.rem(z + Z - 1, Z)}

    def plane(yy, xx, cc):
        return {"src": lax.rem(yy, 4) * 8 + lax.rem(xx, 4) * 2 + cc}

    xp, xm, yp, ym = plane(y, x + 1, c), plane(y, x + 3, c), plane(y + 1, x, c), plane(y + 3, x, c)
    sib = plane(y, x, 1 - c)

    barrier = pltpu.get_barrier_semaphore()
    for d in PARTNERS:
        pl.semaphore_signal(barrier, inc=1, device_id={"rows": lax.rem(z + d, Z)}, device_id_type=MESH)
    for where in (xp, xm, yp, ym, sib):
        pl.semaphore_signal(barrier, inc=1, device_id=where, device_id_type=MESH)

    loads = [
        pltpu.make_async_copy(a, b, in_sem.at[i])
        for i, (a, b) in enumerate(((x_hbm, x_ref), (u_hbm, u_ref), (v_hbm, v_ref), (d_hbm, d_ref)))
    ]
    for load in loads:
        load.start()
    for load in loads[:3]:
        load.wait()

    o = [order_ref[2 * z], order_ref[2 * z + 1]]

    def build(h, _):
        rows, cols = pl.ds(lax.rem(h, 8) * 64, 64), pl.ds((h // 8) * 256, 256)
        x0, x1 = x_ref[0, rows, cols], x_ref[1, rows, cols]
        for k in range(4):
            sel[h, k] = jnp.where(o[0] == k, x0, jnp.where(o[1] == k, x1, jnp.zeros_like(x0)))
        return 0

    lax.fori_loop(0, Z, build, 0)
    wr[0] = sel[lax.rem(z + 8, Z)]
    wl[0] = sel[lax.rem(z + Z - 7, Z)]

    lanes = lax.broadcasted_iota(jnp.int32, (16, 384), 1)
    vm = []
    for s in range(2):
        for k in range(4):
            n = s * 4 + k
            limit = jnp.where(o[s] > k, rank_ref[s, k], 0)
            masked = jnp.where(lanes < limit, v_ref[s, k].astype(jnp.float32), 0.0).astype(jnp.bfloat16)
            g[n, y, x, c] = u_ref[s, k]
            g[8 + n, y, x, c] = masked
            vm.append(masked)
    for p, (j, k) in enumerate(PAIRS):
        zero = jnp.zeros((16, 384), jnp.bfloat16)
        pts[p] = jnp.where(o[0] == j, u_ref[0, k], jnp.where(o[1] == j, u_ref[1, k], zero))
        pts[6 + p] = jnp.where(o[0] == j, vm[k], jnp.where(o[1] == j, vm[4 + k], zero))

    pl.semaphore_wait(barrier, len(PARTNERS) + 5)

    def trio(m):
        return pl.ds(3 * m, 3)

    def near_copy(d):
        m = lax.rem(member + d, 4)
        return remote(pts.at[trio(m)], near.at[member], n_s.at[m], n_r.at[member], {"rows": 4 * group + m})

    def near_in(d):
        m = lax.rem(member + d, 4)
        return remote(near.at[m], near.at[m], n_s.at[m], n_r.at[m], {"rows": 4 * group + m})

    def far_copy(i):
        return remote(mid.at[i], far.at[group], f_s.at[i], f_r.at[group], {"rows": 4 * i + member})

    def far_in(i):
        return remote(far.at[i], far.at[i], f_s.at[0], f_r.at[i], {"rows": 4 * i + member})

    def back_copy(d):
        i = lax.rem(group + d, 4)
        piece = pt.at[3 * member + group, y, x, c]
        return remote(piece, piece, b_s.at[i], b_r.at[group], {"rows": 4 * i + member})

    def back_in(i):
        piece = pt.at[3 * member + i, y, x, c]
        return remote(piece, piece, b_s.at[0], b_r.at[i], {"rows": 4 * i + member})

    def all_copy(d):
        m = lax.rem(member + d, 4)
        pieces = pt.at[trio(member), y, x, c]
        return remote(pieces, pieces, a_s.at[m], a_r.at[member], {"rows": 4 * group + m})

    def all_in(d):
        m = lax.rem(member + d, 4)
        pieces = pt.at[trio(m), y, x, c]
        return remote(pieces, pieces, a_s.at[m], a_r.at[m], {"rows": 4 * group + m})

    def other(i, do):
        @pl.when(i != group)
        def _():
            do(i)

    def tiles_near():
        for d in (2, 1, 3):
            near_copy(d).start()

    def tiles_far():
        near[member] = pts[trio(member)]
        for d in (1, 2, 3):
            near_in(d).wait_recv()
        mid[...] = (near[0] + near[1]) + (near[2] + near[3])
        for i in range(3):
            other(i, lambda i: far_copy(i).start())

    def tiles_back():
        @pl.when(group < 3)
        def _():
            far[group] = mid[group]
            for i in range(4):
                other(i, lambda i: far_in(i).wait_recv())
            pt[3 * member + group, y, x, c] = (far[0] + far[1]) + (far[2] + far[3])
            for d in (2, 1, 3):
                back_copy(d).start()

    def tiles_all():
        for i in range(3):
            other(i, lambda i: back_in(i).wait_recv())
        for d in (2, 1, 3):
            all_copy(d).start()

    def tiles_in():
        for d in (1, 2, 3):
            all_in(d).wait_recv()

    def tiles_done():
        for d in (1, 2, 3):
            near_copy(d).wait_send()
            all_copy(d).wait_send()
        for i in range(3):
            other(i, lambda i: far_copy(i).wait_send())

        @pl.when(group < 3)
        def _():
            for d in (1, 2, 3):
                back_copy(d).wait_send()

    class Gather:
        def __init__(self, buf, n, send, recv):
            self.buf, self.n, self.send, self.recv = buf, n, send, recv

        def part(self, i, lo, hi):
            return pl.ds(i * self.n + lo, hi - lo)

        def bundle(self, i, tiles, stage, yy, xx):
            if stage == 0:
                return self.buf.at[tiles, lax.rem(yy, 4), lax.rem(xx, 4), c]
            if i == 0:
                return self.buf.at[tiles, lax.rem(yy, 4), :, c]
            return self.buf.at[tiles, :, lax.rem(xx, 4), c]

        def copies(self, stage, relay):
            n, half, out = self.n, self.n // 2, []
            for i in range(2):
                along_x = (i == 0) == (stage == 0)
                plus, minus = (xp, xm) if along_x else (yp, ym)
                for d in range(2):
                    where = (plus, minus)[d]
                    back = 1 if d == 0 else -1
                    if relay:
                        tiles = self.part(i, 0, half) if d == 0 else self.part(i, half, n)
                        off_out, off_in = -back, -2 * back
                    else:
                        tiles = self.part(i, 0, n)
                        off_out, off_in = 0, -back
                    yo, xo = (y, x + off_out + 4) if along_x else (y + off_out + 4, x)
                    yi, xi = (y, x + off_in + 4) if along_x else (y + off_in + 4, x)
                    src = self.bundle(i, tiles, stage, yo, xo)
                    dst = self.bundle(i, tiles, stage, yi, xi)
                    slot = ((stage * 2 + relay) * 2 + i) * 2 + d
                    out.append((src, dst, slot, where))
            return out

        def start(self, stage, relay):
            for src, _, slot, where in self.copies(stage, relay):
                remote(src, src, self.send.at[slot], self.recv.at[slot], where).start()

        def wait(self, stage, relay):
            for _, dst, slot, where in self.copies(stage, relay):
                remote(dst, dst, self.send.at[slot], self.recv.at[slot], where).wait_recv()

        def wait_sends(self):
            for stage in range(2):
                for relay in range(2):
                    for src, _, slot, where in self.copies(stage, relay):
                        remote(src, src, self.send.at[slot], self.recv.at[slot], where).wait_send()
            self.sibling(c).wait_send()

        def sibling(self, core):
            whole = self.buf.at[:, :, :, core]
            return remote(whole, whole, self.send.at[16], self.recv.at[16], sib)

    own, panel = Gather(g, 8, g_s, g_r), Gather(pt, 6, p_s, p_r)

    def rs_right(t, u):
        return remote(wr.at[t, u], wr.at[t + 1, u], rs_sr.at[t, u], rs_rr.at[t, u], right)

    def rs_left(t, u):
        return remote(wl.at[t, u], wl.at[t + 1, u], rs_sl.at[t, u], rs_rl.at[t, u], left)

    def rs_step(t, _):
        hr, hl = lax.rem(z + 8 - t + Z, Z), lax.rem(z + Z - 7 + t, Z)
        for u in range(SUB):
            rs_right(t - 1, u).wait_recv()
            wr[t, u] = wr[t, u] + sel[hr, u]
            rs_right(t, u).start()

            @pl.when(t < RSL)
            def _():
                rs_left(t - 1, u).wait_recv()
                wl[t, u] = wl[t, u] + sel[hl, u]
                rs_left(t, u).start()
        return 0

    def ag_right(t, u):
        piece = r.at[lax.rem(z + Z - t, Z), u]
        return remote(piece, piece, ag_sr.at[t, u], ag_rr.at[t, u], right)

    def ag_left(t, u):
        piece = r.at[lax.rem(z + t, Z), u]
        return remote(piece, piece, ag_sl.at[t, u], ag_rl.at[t, u], left)

    def ag_right_in(t, u):
        piece = r.at[lax.rem(z + Z - t - 1, Z), u]
        return remote(piece, piece, ag_sr.at[t, u], ag_rr.at[t, u], right)

    def ag_left_in(t, u):
        piece = r.at[lax.rem(z + t + 1, Z), u]
        return remote(piece, piece, ag_sl.at[t, u], ag_rl.at[t, u], left)

    def ag_step(t, _):
        for u in range(SUB):
            ag_right_in(t - 1, u).wait_recv()
            ag_right(t, u).start()

            @pl.when(t < RSL)
            def _():
                ag_left_in(t - 1, u).wait_recv()
                ag_left(t, u).start()
        return 0

    def steps(step, lo, hi):
        lax.fori_loop(lo, hi, step, 0)

    tiles_near()
    for u in range(SUB):
        rs_right(0, u).start()
        rs_left(0, u).start()
    own.start(0, 0)
    steps(rs_step, 1, 2)
    tiles_far()
    own.wait(0, 0)
    own.start(0, 1)
    steps(rs_step, 2, 4)
    tiles_back()
    own.wait(0, 1)
    own.start(1, 0)
    steps(rs_step, 4, 6)
    tiles_all()
    steps(rs_step, 6, 8)
    for u in range(SUB):
        rs_right(RSR - 1, u).wait_recv()
        rs_left(RSL - 1, u).wait_recv()
        r[z, u] = sel[z, u] + wr[RSR, u] + wl[RSL, u]
        ag_right(0, u).start()
        ag_left(0, u).start()
    tiles_in()
    panel.start(0, 0)
    own.wait(1, 0)
    own.start(1, 1)
    steps(ag_step, 1, 2)
    panel.wait(0, 0)
    panel.start(0, 1)
    steps(ag_step, 2, 3)
    panel.wait(0, 1)
    panel.start(1, 0)
    own.wait(1, 1)
    own.sibling(c).start()
    steps(ag_step, 3, 5)
    panel.wait(1, 0)
    panel.start(1, 1)
    steps(ag_step, 5, 6)
    own.sibling(1 - c).wait_recv()
    panel.wait(1, 1)
    panel.sibling(c).start()
    steps(ag_step, 6, 8)
    for u in range(SUB):
        ag_left_in(RSL - 1, u).wait_recv()
    panel.sibling(1 - c).wait_recv()
    loads[3].wait()

    def tile(ref, n):
        return ref[n].reshape(512, 384)

    def couple(v, value):
        return lax.dot_general(v, value, (((0,), (0,)), ((), ())), preferred_element_type=jnp.float32).astype(jnp.bfloat16)

    def solve(half, _):
        @pl.when(half == 1)
        def _():
            for u in range(SUB):
                ag_right_in(RSR - 1, u).wait_recv()

        i = lax.rem(z // 8 + half, 2)

        def block(k):
            return jnp.concatenate([r[8 * i + q, k] for q in range(8)], axis=0)

        cols = pl.ds(pl.multiple_of(i * 256, 256), 256)
        for k in range(4):
            current = block(k)
            if k > 0:
                acc = current.astype(jnp.float32)
                for j in range(k):
                    p = PAIRS.index((k, j))
                    term = couple(tile(pt, 6 + p), ys[j])
                    acc = acc - jnp.dot(tile(pt, p), term, preferred_element_type=jnp.float32)
                current = acc.astype(jnp.bfloat16)
            ys[k] = jnp.dot(d_ref[k], current, preferred_element_type=jnp.float32).astype(jnp.bfloat16)
            psv_ref[k, :, cols] = ys[k, pl.ds(pl.multiple_of(z * 32, 32), 32), :]
        for s in range(2):
            acc = x_ref[s, :, cols].astype(jnp.float32)
            for k in range(4):
                term = couple(tile(g, 8 + s * 4 + k), ys[k])
                acc = acc - jnp.dot(tile(g, s * 4 + k), term, preferred_element_type=jnp.float32)
            out_ref[s, :, cols] = acc.astype(jnp.bfloat16)
        return 0

    lax.fori_loop(0, 2, solve, 0)

    def rs_done(t, _):
        for u in range(SUB):
            rs_right(t, u).wait_send()
            ag_right(t, u).wait_send()

            @pl.when(t < RSL)
            def _():
                rs_left(t, u).wait_send()
                ag_left(t, u).wait_send()
        return 0

    lax.fori_loop(0, RSR, rs_done, 0)
    tiles_done()
    own.wait_sends()
    panel.wait_sends()


def finish_kernel(psv_in, out_in, psv_ref, out_ref):
    psv_ref[...] = psv_in[...]
    out_ref[...] = out_in[...]


def local(right_side, diag_inverse, factor_u, factor_v, tile_rank, block_order):
    vmem = pl.BlockSpec(memory_space=pltpu.VMEM)
    smem = pl.BlockSpec(memory_space=pltpu.SMEM)
    anywhere = pl.BlockSpec(memory_space=pl.ANY)
    bf16 = jnp.bfloat16
    dma = pltpu.SemaphoreType.DMA
    results = (
        jax.ShapeDtypeStruct((4, 32, 512), bf16),
        jax.ShapeDtypeStruct((2, 512, 512), bf16),
    )
    solved = pl.pallas_call(
        kernel,
        out_shape=results,
        in_specs=[smem, smem] + [anywhere] * 4,
        out_specs=(vmem, vmem),
        scratch_shapes=[
            pltpu.VMEM((2, 512, 512), bf16),
            pltpu.VMEM((4, 512, 512), bf16),
            pltpu.VMEM((2, 4, 16, 384), bf16),
            pltpu.VMEM((2, 4, 16, 384), bf16),
            pltpu.VMEM((Z, 4, 64, 256), bf16),
            pltpu.VMEM((RSR + 1, 4, 64, 256), bf16),
            pltpu.VMEM((RSL + 1, 4, 64, 256), bf16),
            pltpu.VMEM((Z, 4, 64, 256), bf16),
            pltpu.VMEM((16, 4, 4, 2, 16, 384), bf16),
            pltpu.VMEM((12, 4, 4, 2, 16, 384), bf16),
            pltpu.VMEM((12, 16, 384), bf16),
            pltpu.VMEM((4, 3, 16, 384), bf16),
            pltpu.VMEM((3, 16, 384), bf16),
            pltpu.VMEM((4, 16, 384), bf16),
            pltpu.VMEM((4, 512, 256), bf16),
            dma((4,)),
            dma((RSR, SUB)), dma((RSR, SUB)), dma((RSL, SUB)), dma((RSL, SUB)),
            dma((RSR, SUB)), dma((RSR, SUB)), dma((RSL, SUB)), dma((RSL, SUB)),
            dma((4,)), dma((4,)), dma((4,)), dma((4,)), dma((4,)), dma((4,)), dma((4,)), dma((4,)),
            dma((17,)), dma((17,)), dma((17,)), dma((17,)),
        ],
        compiler_params=pltpu.CompilerParams(
            collective_id=0, has_side_effects=True, vmem_limit_bytes=56 * 2**20
        ),
        cost_estimate=pl.CostEstimate(flops=7_000_000_000, bytes_accessed=8_000_000, transcendentals=0),
    )(block_order, tile_rank, right_side, diag_inverse, factor_u, factor_v)
    return pl.pallas_call(finish_kernel, out_shape=results)(*solved)


def solution(mesh):
    placed = (
        P("rows", None, "src"),
        P(),
        P("rows", None, "src", None),
        P("rows", None, "src", None),
        P("rows", None),
        P(),
    )
    return jax.shard_map(
        local,
        mesh=mesh,
        in_specs=placed,
        out_specs=(P(None, "rows", "src"), P("rows", None, "src")),
        check_vma=False,
    )
```

```python
import functools

import jax
import jax.numpy as jnp
from jax import lax
from jax.experimental import pallas as pl
from jax.experimental.pallas import tpu as pltpu
from jax.sharding import PartitionSpec as P

MESH = pl.DeviceIdType.MESH
PAIRS = ((1, 0), (2, 0), (2, 1), (3, 0), (3, 1), (3, 2))
Z = 16
SUB = 4
PARTNERS = (1, 2, 3, 4, 8, 12, 13, 14, 15)
RSR, RSL = 8, 7


def remote(src, dst, send, recv, where):
    return pltpu.make_async_remote_copy(
        src_ref=src, dst_ref=dst, send_sem=send, recv_sem=recv, device_id=where, device_id_type=MESH
    )


def kernel(
    order_ref, rank_ref, x_hbm, d_hbm, u_hbm, v_hbm,
    psv_ref, out_ref,
    x_ref, d_ref, u_ref, v_ref, sel, wr, wl, r, g, pt, pts, near, mid, far, tg, tp, ys,
    in_sem, rs_sr, rs_rr, rs_sl, rs_rl, ag_sr, ag_rr, ag_sl, ag_rl,
    n_s, n_r, f_s, f_r, b_s, b_r, a_s, a_r, g_s, g_r, p_s, p_r,
):
    z = lax.axis_index("rows")
    me = lax.axis_index("src")
    y, x, c = me // 8, lax.rem(me // 2, 4), lax.rem(me, 2)
    group, member = z // 4, lax.rem(z, 4)
    turn = 1 - 2 * c

    def at(d):
        return lax.rem(z + turn * d + Z, Z)

    right, left = {"rows": at(1)}, {"rows": at(-1)}

    def plane(yy, xx, cc):
        return {"src": lax.rem(yy, 4) * 8 + lax.rem(xx, 4) * 2 + cc}

    xp, xm, yp, ym = plane(y, x + 1, c), plane(y, x + 3, c), plane(y + 1, x, c), plane(y + 3, x, c)
    sib = plane(y, x, 1 - c)

    barrier = pltpu.get_barrier_semaphore()
    for d in PARTNERS:
        pl.semaphore_signal(barrier, inc=1, device_id={"rows": lax.rem(z + d, Z)}, device_id_type=MESH)
    for where in (xp, xm, yp, ym, sib):
        pl.semaphore_signal(barrier, inc=1, device_id=where, device_id_type=MESH)

    loads = [
        pltpu.make_async_copy(a, b, in_sem.at[i])
        for i, (a, b) in enumerate(((x_hbm, x_ref), (u_hbm, u_ref), (v_hbm, v_ref), (d_hbm, d_ref)))
    ]
    for load in loads:
        load.start()
    for load in loads[:3]:
        load.wait()

    o = [order_ref[2 * z], order_ref[2 * z + 1]]

    def build(h, _):
        rows, cols = pl.ds(lax.rem(h, 4) * 128, 128), pl.ds((h // 4) * 128, 128)
        x0, x1 = x_ref[0, rows, cols], x_ref[1, rows, cols]
        for k in range(4):
            sel[h, k] = jnp.where(o[0] == k, x0, jnp.where(o[1] == k, x1, jnp.zeros_like(x0)))
        return 0

    lax.fori_loop(0, Z, build, 0)
    wr[0] = sel[at(8)]
    wl[0] = sel[at(-7)]

    lanes = lax.broadcasted_iota(jnp.int32, (16, 384), 1)
    vm = []
    for s in range(2):
        for k in range(4):
            n = s * 4 + k
            limit = jnp.where(o[s] > k, rank_ref[s, k], 0)
            masked = jnp.where(lanes < limit, v_ref[s, k].astype(jnp.float32), 0.0).astype(jnp.bfloat16)
            g[n, y, x, c] = u_ref[s, k]
            g[8 + n, y, x, c] = masked
            vm.append(masked)
    for p, (j, k) in enumerate(PAIRS):
        zero = jnp.zeros((16, 384), jnp.bfloat16)
        pts[p] = jnp.where(o[0] == j, u_ref[0, k], jnp.where(o[1] == j, u_ref[1, k], zero))
        pts[6 + p] = jnp.where(o[0] == j, vm[k], jnp.where(o[1] == j, vm[4 + k], zero))

    pl.semaphore_wait(barrier, len(PARTNERS) + 5)

    def trio(m):
        return pl.ds(3 * m, 3)

    def near_copy(d):
        m = lax.rem(member + d, 4)
        return remote(pts.at[trio(m)], near.at[member], n_s.at[m], n_r.at[member], {"rows": 4 * group + m})

    def near_in(d):
        m = lax.rem(member + d, 4)
        return remote(near.at[m], near.at[m], n_s.at[m], n_r.at[m], {"rows": 4 * group + m})

    def far_copy(i):
        return remote(mid.at[i], far.at[group], f_s.at[i], f_r.at[group], {"rows": 4 * i + member})

    def far_in(i):
        return remote(far.at[i], far.at[i], f_s.at[0], f_r.at[i], {"rows": 4 * i + member})

    def back_copy(d):
        i = lax.rem(group + d, 4)
        piece = pt.at[3 * member + group, y, x, c]
        return remote(piece, piece, b_s.at[i], b_r.at[group], {"rows": 4 * i + member})

    def back_in(i):
        piece = pt.at[3 * member + i, y, x, c]
        return remote(piece, piece, b_s.at[0], b_r.at[i], {"rows": 4 * i + member})

    def all_copy(d):
        m = lax.rem(member + d, 4)
        pieces = pt.at[trio(member), y, x, c]
        return remote(pieces, pieces, a_s.at[m], a_r.at[member], {"rows": 4 * group + m})

    def all_in(d):
        m = lax.rem(member + d, 4)
        pieces = pt.at[trio(m), y, x, c]
        return remote(pieces, pieces, a_s.at[m], a_r.at[m], {"rows": 4 * group + m})

    def other(i, do):
        @pl.when(i != group)
        def _():
            do(i)

    def tiles_near():
        for d in (2, 1, 3):
            near_copy(d).start()

    def tiles_far():
        near[member] = pts[trio(member)]
        for d in (1, 2, 3):
            near_in(d).wait_recv()
        mid[...] = (near[0] + near[1]) + (near[2] + near[3])
        for i in range(3):
            other(i, lambda i: far_copy(i).start())

    def tiles_back():
        @pl.when(group < 3)
        def _():
            far[group] = mid[group]
            for i in range(4):
                other(i, lambda i: far_in(i).wait_recv())
            pt[3 * member + group, y, x, c] = (far[0] + far[1]) + (far[2] + far[3])
            for d in (2, 1, 3):
                back_copy(d).start()

    def tiles_all():
        for i in range(3):
            other(i, lambda i: back_in(i).wait_recv())
        for d in (2, 1, 3):
            all_copy(d).start()

    def tiles_in():
        for d in (1, 2, 3):
            all_in(d).wait_recv()

    def tiles_done():
        for d in (1, 2, 3):
            near_copy(d).wait_send()
            all_copy(d).wait_send()
        for i in range(3):
            other(i, lambda i: far_copy(i).wait_send())

        @pl.when(group < 3)
        def _():
            for d in (1, 2, 3):
                back_copy(d).wait_send()

    class Gather:
        def __init__(self, buf, n, send, recv, pieces):
            self.buf, self.n, self.send, self.recv, self.pieces = buf, n, send, recv, pieces

        def part(self, i, lo, hi):
            return pl.ds(i * self.n + lo, hi - lo)

        def bundle(self, i, tiles, stage, yy, xx):
            if stage == 0:
                return self.buf.at[tiles, lax.rem(yy, 4), lax.rem(xx, 4), c]
            if i == 0:
                return self.buf.at[tiles, lax.rem(yy, 4), :, c]
            return self.buf.at[tiles, :, lax.rem(xx, 4), c]

        def copies(self, stage, relay):
            n, half, out = self.n, self.n // 2, []
            for i in range(2):
                along_x = (i == 0) == (stage == 0)
                plus, minus = (xp, xm) if along_x else (yp, ym)
                for d in range(2):
                    where = (plus, minus)[d]
                    back = 1 if d == 0 else -1
                    if relay:
                        tiles = self.part(i, 0, half) if d == 0 else self.part(i, half, n)
                        off_out, off_in = -back, -2 * back
                    else:
                        tiles = self.part(i, 0, n)
                        off_out, off_in = 0, -back
                    yo, xo = (y, x + off_out + 4) if along_x else (y + off_out + 4, x)
                    yi, xi = (y, x + off_in + 4) if along_x else (y + off_in + 4, x)
                    src = self.bundle(i, tiles, stage, yo, xo)
                    dst = self.bundle(i, tiles, stage, yi, xi)
                    slot = ((stage * 2 + relay) * 2 + i) * 2 + d
                    out.append((src, dst, slot, where))
            return out

        def start(self, stage, relay):
            for src, _, slot, where in self.copies(stage, relay):
                remote(src, src, self.send.at[slot], self.recv.at[slot], where).start()

        def wait(self, stage, relay):
            for _, dst, slot, where in self.copies(stage, relay):
                remote(dst, dst, self.send.at[slot], self.recv.at[slot], where).wait_recv()

        def wait_sends(self):
            for stage in range(2):
                for relay in range(2):
                    for src, _, slot, where in self.copies(stage, relay):
                        remote(src, src, self.send.at[slot], self.recv.at[slot], where).wait_send()
            if self.pieces:
                for d in range(4):
                    self.sibling_piece(d, c, "wait_send")
            else:
                self.sibling(c).wait_send()

        def sibling_piece(self, d, core, act):
            for i in range(2):
                tiles = self.part(i, 0, self.n)
                if i == 0:
                    piece = self.buf.at[tiles, lax.rem(y + d, 4), :, core]
                else:
                    piece = self.buf.at[tiles, :, lax.rem(x + d, 4), core]
                slot = 16 + 2 * d + i
                getattr(remote(piece, piece, self.send.at[slot], self.recv.at[slot], sib), act)()

        def sibling(self, core):
            whole = self.buf.at[:, :, :, core]
            return remote(whole, whole, self.send.at[16], self.recv.at[16], sib)

    own, panel = Gather(g, 8, g_s, g_r, False), Gather(pt, 6, p_s, p_r, True)

    def rs_right(t, u):
        return remote(wr.at[t, u], wr.at[t + 1, u], rs_sr.at[t, u], rs_rr.at[t, u], right)

    def rs_left(t, u):
        return remote(wl.at[t, u], wl.at[t + 1, u], rs_sl.at[t, u], rs_rl.at[t, u], left)

    def rs_step(t, _):
        hr, hl = at(8 - t), at(t - 7)
        for u in range(SUB):
            rs_right(t - 1, u).wait_recv()
            wr[t, u] = wr[t, u] + sel[hr, u]
            rs_right(t, u).start()

            @pl.when(t < RSL)
            def _():
                rs_left(t - 1, u).wait_recv()
                wl[t, u] = wl[t, u] + sel[hl, u]
                rs_left(t, u).start()
        return 0

    def ag_right(t, u):
        piece = r.at[at(-t), u]
        return remote(piece, piece, ag_sr.at[t, u], ag_rr.at[t, u], right)

    def ag_left(t, u):
        piece = r.at[at(t), u]
        return remote(piece, piece, ag_sl.at[t, u], ag_rl.at[t, u], left)

    def ag_right_in(t, u):
        piece = r.at[at(-t - 1), u]
        return remote(piece, piece, ag_sr.at[t, u], ag_rr.at[t, u], right)

    def ag_left_in(t, u):
        piece = r.at[at(t + 1), u]
        return remote(piece, piece, ag_sl.at[t, u], ag_rl.at[t, u], left)

    def ag_step(t, _):
        for u in range(SUB):
            ag_right_in(t - 1, u).wait_recv()
            ag_right(t, u).start()

            @pl.when(t < RSL)
            def _():
                ag_left_in(t - 1, u).wait_recv()
                ag_left(t, u).start()
        return 0

    def tile(ref, n):
        return ref[n].reshape(512, 384)

    def product(left_factor, right_factor):
        whole = lax.dot_general(
            left_factor, right_factor, (((1,), (1,)), ((), ())), preferred_element_type=jnp.float32
        )
        return whole.astype(jnp.bfloat16)

    def own_products(n, _):
        tg[n // 4, :, pl.ds(pl.multiple_of(lax.rem(n, 4) * 512, 512), 512)] = product(tile(g, n), tile(g, 8 + n))
        return 0

    def panel_products():
        for p, (j, k) in enumerate(PAIRS):
            tp[j - 1, :, k * 512 : (k + 1) * 512] = product(tile(pt, p), tile(pt, 6 + p))

    first = lax.rem(group + jnp.where(member < 2, 3, 0), 4)

    def quarters(part):
        return [lax.rem(first + 2 * part + a, 4) for a in range(2)]

    def columns(i):
        return pl.ds(pl.multiple_of(i * 128, 128), 128)

    def solve(part):
        pair = quarters(part)

        def block(k):
            return jnp.concatenate(
                [jnp.concatenate([r[4 * i + q, k] for q in range(4)], axis=0) for i in pair], axis=1
            )

        for k in range(4):
            current = block(k)
            if k > 0:
                known = k * 512
                term = jnp.dot(tp[k - 1, :, :known], ys[:known], preferred_element_type=jnp.float32)
                current = (current.astype(jnp.float32) - term).astype(jnp.bfloat16)
            ys[k * 512 : (k + 1) * 512] = jnp.dot(
                d_ref[k], current, preferred_element_type=jnp.float32
            ).astype(jnp.bfloat16)
            mine = ys[pl.ds(pl.multiple_of(k * 512 + z * 32, 32), 32), :]
            for a, i in enumerate(pair):
                psv_ref[k, :, columns(i)] = mine[:, a * 128 : (a + 1) * 128]

    def update(part):
        pair = quarters(part)
        for s in range(2):
            acc = jnp.concatenate([x_ref[s, :, columns(i)] for i in pair], axis=1).astype(jnp.float32)
            acc = acc - jnp.dot(tg[s], ys[...], preferred_element_type=jnp.float32)
            acc = acc.astype(jnp.bfloat16)
            for a, i in enumerate(pair):
                out_ref[s, :, columns(i)] = acc[:, a * 128 : (a + 1) * 128]

    def steps(step, lo, hi):
        lax.fori_loop(lo, hi, step, 0)

    tiles_near()
    for u in range(SUB):
        rs_right(0, u).start()
        rs_left(0, u).start()
    own.start(0, 0)
    tiles_far()
    steps(rs_step, 1, 3)
    own.wait(0, 0)
    own.start(0, 1)
    tiles_back()
    steps(rs_step, 3, 4)
    own.wait(0, 1)
    own.start(1, 0)
    steps(rs_step, 4, 5)
    tiles_all()
    steps(rs_step, 5, 6)
    own.wait(1, 0)
    own.start(1, 1)
    steps(rs_step, 6, 7)
    tiles_in()
    panel.start(0, 0)
    steps(rs_step, 7, 8)
    for u in range(SUB):
        rs_right(RSR - 1, u).wait_recv()
        rs_left(RSL - 1, u).wait_recv()
        r[z, u] = sel[z, u] + wr[RSR, u] + wl[RSL, u]
        ag_right(0, u).start()
        ag_left(0, u).start()
    panel.wait(0, 0)
    panel.start(0, 1)
    own.wait(1, 1)
    own.sibling(c).start()
    steps(ag_step, 1, 2)
    panel.wait(0, 1)
    panel.start(1, 0)
    panel.sibling_piece(0, c, "start")
    steps(ag_step, 2, 3)
    own.sibling(1 - c).wait_recv()
    lax.fori_loop(0, 2, own_products, 0)
    steps(ag_step, 3, 4)
    panel.wait(1, 0)
    panel.start(1, 1)
    panel.sibling_piece(1, c, "start")
    panel.sibling_piece(3, c, "start")
    lax.fori_loop(2, 4, own_products, 0)
    steps(ag_step, 4, 5)
    lax.fori_loop(4, 6, own_products, 0)
    steps(ag_step, 5, 6)
    panel.wait(1, 1)
    panel.sibling_piece(2, c, "start")
    lax.fori_loop(6, 8, own_products, 0)
    steps(ag_step, 6, 7)
    for d in range(4):
        panel.sibling_piece(d, 1 - c, "wait_recv")
    loads[3].wait()
    panel_products()
    steps(ag_step, 7, 8)
    solve(0)
    update(0)
    for u in range(SUB):
        ag_right_in(RSR - 1, u).wait_recv()
        ag_left_in(RSL - 1, u).wait_recv()
    solve(1)
    update(1)

    def rs_done(t, _):
        for u in range(SUB):
            rs_right(t, u).wait_send()
            ag_right(t, u).wait_send()

            @pl.when(t < RSL)
            def _():
                rs_left(t, u).wait_send()
                ag_left(t, u).wait_send()
        return 0

    lax.fori_loop(0, RSR, rs_done, 0)
    tiles_done()
    own.wait_sends()
    panel.wait_sends()


def finish_kernel(psv_in, out_in, psv_ref, out_ref):
    psv_ref[...] = psv_in[...]
    out_ref[...] = out_in[...]


def local(right_side, diag_inverse, factor_u, factor_v, tile_rank, block_order):
    vmem = pl.BlockSpec(memory_space=pltpu.VMEM)
    smem = pl.BlockSpec(memory_space=pltpu.SMEM)
    anywhere = pl.BlockSpec(memory_space=pl.ANY)
    bf16 = jnp.bfloat16
    dma = pltpu.SemaphoreType.DMA
    results = (
        jax.ShapeDtypeStruct((4, 32, 512), bf16),
        jax.ShapeDtypeStruct((2, 512, 512), bf16),
    )
    solved = pl.pallas_call(
        kernel,
        out_shape=results,
        in_specs=[smem, smem] + [anywhere] * 4,
        out_specs=(vmem, vmem),
        scratch_shapes=[
            pltpu.VMEM((2, 512, 512), bf16),
            pltpu.VMEM((4, 512, 512), bf16),
            pltpu.VMEM((2, 4, 16, 384), bf16),
            pltpu.VMEM((2, 4, 16, 384), bf16),
            pltpu.VMEM((Z, 4, 128, 128), bf16),
            pltpu.VMEM((RSR + 1, 4, 128, 128), bf16),
            pltpu.VMEM((RSL + 1, 4, 128, 128), bf16),
            pltpu.VMEM((Z, 4, 128, 128), bf16),
            pltpu.VMEM((16, 4, 4, 2, 16, 384), bf16),
            pltpu.VMEM((12, 4, 4, 2, 16, 384), bf16),
            pltpu.VMEM((12, 16, 384), bf16),
            pltpu.VMEM((4, 3, 16, 384), bf16),
            pltpu.VMEM((3, 16, 384), bf16),
            pltpu.VMEM((4, 16, 384), bf16),
            pltpu.VMEM((2, 512, 2048), bf16),
            pltpu.VMEM((3, 512, 1536), bf16),
            pltpu.VMEM((2048, 256), bf16),
            dma((4,)),
            dma((RSR, SUB)), dma((RSR, SUB)), dma((RSL, SUB)), dma((RSL, SUB)),
            dma((RSR, SUB)), dma((RSR, SUB)), dma((RSL, SUB)), dma((RSL, SUB)),
            dma((4,)), dma((4,)), dma((4,)), dma((4,)), dma((4,)), dma((4,)), dma((4,)), dma((4,)),
            dma((17,)), dma((17,)), dma((24,)), dma((24,)),
        ],
        compiler_params=pltpu.CompilerParams(
            collective_id=0, has_side_effects=True, vmem_limit_bytes=56 * 2**20
        ),
        cost_estimate=pl.CostEstimate(flops=7_000_000_000, bytes_accessed=8_000_000, transcendentals=0),
    )(block_order, tile_rank, right_side, diag_inverse, factor_u, factor_v)
    return pl.pallas_call(finish_kernel, out_shape=results)(*solved)


def solution(mesh):
    placed = (
        P("rows", None, "src"),
        P(),
        P("rows", None, "src", None),
        P("rows", None, "src", None),
        P("rows", None),
        P(),
    )
    return jax.shard_map(
        local,
        mesh=mesh,
        in_specs=placed,
        out_specs=(P(None, "rows", "src"), P("rows", None, "src")),
        check_vma=False,
    )
```

```python
import functools

import jax
import jax.numpy as jnp
from jax import lax
from jax.experimental import pallas as pl
from jax.experimental.pallas import tpu as pltpu
from jax.sharding import PartitionSpec as P

MESH = pl.DeviceIdType.MESH
PAIRS = ((1, 0), (2, 0), (2, 1), (3, 0), (3, 1), (3, 2))
Z = 16
SUB = 4
PARTNERS = (1, 2, 3, 4, 8, 12, 13, 14, 15)
RSR, RSL = 8, 7


def remote(src, dst, send, recv, where):
    return pltpu.make_async_remote_copy(
        src_ref=src, dst_ref=dst, send_sem=send, recv_sem=recv, device_id=where, device_id_type=MESH
    )


def kernel(
    order_ref, rank_ref, x_hbm, d_hbm, u_hbm, v_hbm,
    psv_ref, out_ref,
    x_ref, d_ref, u_ref, v_ref, wr, wl, r, g, pt, pts, near, mid, far, tg, tp, ys,
    in_sem, rs_sr, rs_rr, rs_sl, rs_rl, ag_sr, ag_rr, ag_sl, ag_rl,
    n_s, n_r, f_s, f_r, b_s, b_r, a_s, a_r, g_s, g_r, p_s, p_r,
):
    z = lax.axis_index("rows")
    me = lax.axis_index("src")
    y, x, c = me // 8, lax.rem(me // 2, 4), lax.rem(me, 2)
    group, member = z // 4, lax.rem(z, 4)
    turn = 1 - 2 * c

    def at(d):
        return lax.rem(z + turn * d + Z, Z)

    right, left = {"rows": at(1)}, {"rows": at(-1)}

    def plane(yy, xx, cc):
        return {"src": lax.rem(yy, 4) * 8 + lax.rem(xx, 4) * 2 + cc}

    xp, xm, yp, ym = plane(y, x + 1, c), plane(y, x + 3, c), plane(y + 1, x, c), plane(y + 3, x, c)
    sib = plane(y, x, 1 - c)

    barrier = pltpu.get_barrier_semaphore()
    for d in PARTNERS:
        pl.semaphore_signal(barrier, inc=1, device_id={"rows": lax.rem(z + d, Z)}, device_id_type=MESH)
    for where in (xp, xm, yp, ym, sib):
        pl.semaphore_signal(barrier, inc=1, device_id=where, device_id_type=MESH)

    loads = [
        pltpu.make_async_copy(a, b, in_sem.at[i])
        for i, (a, b) in enumerate(((x_hbm, x_ref), (u_hbm, u_ref), (v_hbm, v_ref), (d_hbm, d_ref)))
    ]
    for load in loads:
        load.start()
    for load in loads[1:3]:
        load.wait()

    o = [order_ref[2 * z], order_ref[2 * z + 1]]

    def pick(h, k):
        rows, cols = pl.ds(lax.rem(h, 4) * 128, 128), pl.ds(pl.multiple_of((h // 4) * 128, 128), 128)
        x0, x1 = x_ref[0, rows, cols], x_ref[1, rows, cols]
        return jnp.where(o[0] == k, x0, jnp.where(o[1] == k, x1, jnp.zeros_like(x0)))

    lanes = lax.broadcasted_iota(jnp.int32, (16, 384), 1)
    vm = []
    for s in range(2):
        for k in range(4):
            n = s * 4 + k
            limit = jnp.where(o[s] > k, rank_ref[s, k], 0)
            masked = jnp.where(lanes < limit, v_ref[s, k].astype(jnp.float32), 0.0).astype(jnp.bfloat16)
            g[n, y, x, c] = u_ref[s, k]
            g[8 + n, y, x, c] = masked
            vm.append(masked)
    for p, (j, k) in enumerate(PAIRS):
        zero = jnp.zeros((16, 384), jnp.bfloat16)
        pts[p] = jnp.where(o[0] == j, u_ref[0, k], jnp.where(o[1] == j, u_ref[1, k], zero))
        pts[6 + p] = jnp.where(o[0] == j, vm[k], jnp.where(o[1] == j, vm[4 + k], zero))

    pl.semaphore_wait(barrier, len(PARTNERS) + 5)

    def trio(m):
        return pl.ds(3 * m, 3)

    def near_copy(d):
        m = lax.rem(member + d, 4)
        return remote(pts.at[trio(m)], near.at[member], n_s.at[m], n_r.at[member], {"rows": 4 * group + m})

    def near_in(d):
        m = lax.rem(member + d, 4)
        return remote(near.at[m], near.at[m], n_s.at[m], n_r.at[m], {"rows": 4 * group + m})

    def far_copy(i):
        return remote(mid.at[i], far.at[group], f_s.at[i], f_r.at[group], {"rows": 4 * i + member})

    def far_in(i):
        return remote(far.at[i], far.at[i], f_s.at[0], f_r.at[i], {"rows": 4 * i + member})

    def back_copy(d):
        i = lax.rem(group + d, 4)
        piece = pt.at[3 * member + group, y, x, c]
        return remote(piece, piece, b_s.at[i], b_r.at[group], {"rows": 4 * i + member})

    def back_in(i):
        piece = pt.at[3 * member + i, y, x, c]
        return remote(piece, piece, b_s.at[0], b_r.at[i], {"rows": 4 * i + member})

    def all_copy(d):
        m = lax.rem(member + d, 4)
        pieces = pt.at[trio(member), y, x, c]
        return remote(pieces, pieces, a_s.at[m], a_r.at[member], {"rows": 4 * group + m})

    def all_in(d):
        m = lax.rem(member + d, 4)
        pieces = pt.at[trio(m), y, x, c]
        return remote(pieces, pieces, a_s.at[m], a_r.at[m], {"rows": 4 * group + m})

    def other(i, do):
        @pl.when(i != group)
        def _():
            do(i)

    def tiles_near():
        for d in (2, 1, 3):
            near_copy(d).start()

    def tiles_far():
        near[member] = pts[trio(member)]
        for d in (1, 2, 3):
            near_in(d).wait_recv()
        mid[...] = (near[0] + near[1]) + (near[2] + near[3])
        for i in range(3):
            other(i, lambda i: far_copy(i).start())

    def tiles_back():
        @pl.when(group < 3)
        def _():
            far[group] = mid[group]
            for i in range(4):
                other(i, lambda i: far_in(i).wait_recv())
            pt[3 * member + group, y, x, c] = (far[0] + far[1]) + (far[2] + far[3])
            for d in (2, 1, 3):
                back_copy(d).start()

    def tiles_all():
        for i in range(3):
            other(i, lambda i: back_in(i).wait_recv())
        for d in (2, 1, 3):
            all_copy(d).start()

    def tiles_in():
        for d in (1, 2, 3):
            all_in(d).wait_recv()

    def tiles_done():
        for d in (1, 2, 3):
            near_copy(d).wait_send()
            all_copy(d).wait_send()
        for i in range(3):
            other(i, lambda i: far_copy(i).wait_send())

        @pl.when(group < 3)
        def _():
            for d in (1, 2, 3):
                back_copy(d).wait_send()

    class Gather:
        def __init__(self, buf, n, send, recv, pieces):
            self.buf, self.n, self.send, self.recv, self.pieces = buf, n, send, recv, pieces

        def part(self, i, lo, hi):
            return pl.ds(i * self.n + lo, hi - lo)

        def bundle(self, i, tiles, stage, yy, xx):
            if stage == 0:
                return self.buf.at[tiles, lax.rem(yy, 4), lax.rem(xx, 4), c]
            if i == 0:
                return self.buf.at[tiles, lax.rem(yy, 4), :, c]
            return self.buf.at[tiles, :, lax.rem(xx, 4), c]

        def copies(self, stage, relay):
            n, half, out = self.n, self.n // 2, []
            for i in range(2):
                along_x = (i == 0) == (stage == 0)
                plus, minus = (xp, xm) if along_x else (yp, ym)
                for d in range(2):
                    where = (plus, minus)[d]
                    back = 1 if d == 0 else -1
                    if relay:
                        tiles = self.part(i, 0, half) if d == 0 else self.part(i, half, n)
                        off_out, off_in = -back, -2 * back
                    else:
                        tiles = self.part(i, 0, n)
                        off_out, off_in = 0, -back
                    yo, xo = (y, x + off_out + 4) if along_x else (y + off_out + 4, x)
                    yi, xi = (y, x + off_in + 4) if along_x else (y + off_in + 4, x)
                    src = self.bundle(i, tiles, stage, yo, xo)
                    dst = self.bundle(i, tiles, stage, yi, xi)
                    slot = ((stage * 2 + relay) * 2 + i) * 2 + d
                    out.append((src, dst, slot, where))
            return out

        def start(self, stage, relay):
            for src, _, slot, where in self.copies(stage, relay):
                remote(src, src, self.send.at[slot], self.recv.at[slot], where).start()

        def wait(self, stage, relay):
            for _, dst, slot, where in self.copies(stage, relay):
                remote(dst, dst, self.send.at[slot], self.recv.at[slot], where).wait_recv()

        def wait_sends(self):
            for stage in range(2):
                for relay in range(2):
                    for src, _, slot, where in self.copies(stage, relay):
                        remote(src, src, self.send.at[slot], self.recv.at[slot], where).wait_send()
            if self.pieces:
                for d in range(4):
                    self.sibling_piece(d, c, "wait_send")
            else:
                self.sibling(c).wait_send()

        def sibling_piece(self, d, core, act):
            for i in range(2):
                tiles = self.part(i, 0, self.n)
                if i == 0:
                    piece = self.buf.at[tiles, lax.rem(y + d, 4), :, core]
                else:
                    piece = self.buf.at[tiles, :, lax.rem(x + d, 4), core]
                slot = 16 + 2 * d + i
                getattr(remote(piece, piece, self.send.at[slot], self.recv.at[slot], sib), act)()

        def sibling(self, core):
            whole = self.buf.at[:, :, :, core]
            return remote(whole, whole, self.send.at[16], self.recv.at[16], sib)

    own, panel = Gather(g, 8, g_s, g_r, False), Gather(pt, 6, p_s, p_r, True)

    def rs_right(t, u):
        return remote(wr.at[t, u], wr.at[t + 1, u], rs_sr.at[t, u], rs_rr.at[t, u], right)

    def rs_left(t, u):
        return remote(wl.at[t, u], wl.at[t + 1, u], rs_sl.at[t, u], rs_rl.at[t, u], left)

    def rs_step(t, _):
        hr, hl = at(8 - t), at(t - 7)
        for u in range(SUB):
            rs_right(t - 1, u).wait_recv()
            wr[t, u] = wr[t, u] + pick(hr, u)
            rs_right(t, u).start()

            @pl.when(t < RSL)
            def _():
                rs_left(t - 1, u).wait_recv()
                wl[t, u] = wl[t, u] + pick(hl, u)
                rs_left(t, u).start()
        return 0

    def ag_right(t, u):
        piece = r.at[at(-t), u]
        return remote(piece, piece, ag_sr.at[t, u], ag_rr.at[t, u], right)

    def ag_left(t, u):
        piece = r.at[at(t), u]
        return remote(piece, piece, ag_sl.at[t, u], ag_rl.at[t, u], left)

    def ag_right_in(t, u):
        piece = r.at[at(-t - 1), u]
        return remote(piece, piece, ag_sr.at[t, u], ag_rr.at[t, u], right)

    def ag_left_in(t, u):
        piece = r.at[at(t + 1), u]
        return remote(piece, piece, ag_sl.at[t, u], ag_rl.at[t, u], left)

    def ag_step(t, _):
        for u in range(SUB):
            ag_right_in(t - 1, u).wait_recv()
            ag_right(t, u).start()

            @pl.when(t < RSL)
            def _():
                ag_left_in(t - 1, u).wait_recv()
                ag_left(t, u).start()
        return 0

    def tile(ref, n):
        return ref[n].reshape(512, 384)

    def product(left_factor, right_factor):
        whole = lax.dot_general(
            left_factor, right_factor, (((1,), (1,)), ((), ())), preferred_element_type=jnp.float32
        )
        return whole.astype(jnp.bfloat16)

    def own_products(n, _):
        tg[n // 4, :, pl.ds(pl.multiple_of(lax.rem(n, 4) * 512, 512), 512)] = product(tile(g, n), tile(g, 8 + n))
        return 0

    def panel_products():
        for p, (j, k) in enumerate(PAIRS):
            tp[j - 1, :, k * 512 : (k + 1) * 512] = product(tile(pt, p), tile(pt, 6 + p))

    first = lax.rem(group + jnp.where(member < 2, 3, 0), 4)

    def quarters(part):
        return [lax.rem(first + 2 * part + a, 4) for a in range(2)]

    def columns(i):
        return pl.ds(pl.multiple_of(i * 128, 128), 128)

    def solve(part):
        pair = quarters(part)

        def block(k):
            return jnp.concatenate(
                [jnp.concatenate([r[4 * i + q, k] for q in range(4)], axis=0) for i in pair], axis=1
            )

        for k in range(4):
            current = block(k)
            if k > 0:
                known = k * 512
                term = jnp.dot(tp[k - 1, :, :known], ys[:known], preferred_element_type=jnp.float32)
                current = (current.astype(jnp.float32) - term).astype(jnp.bfloat16)
            ys[k * 512 : (k + 1) * 512] = jnp.dot(
                d_ref[k], current, preferred_element_type=jnp.float32
            ).astype(jnp.bfloat16)
            mine = ys[pl.ds(pl.multiple_of(k * 512 + z * 32, 32), 32), :]
            for a, i in enumerate(pair):
                psv_ref[k, :, columns(i)] = mine[:, a * 128 : (a + 1) * 128]

    def update(part):
        pair = quarters(part)
        for s in range(2):
            acc = jnp.concatenate([x_ref[s, :, columns(i)] for i in pair], axis=1).astype(jnp.float32)
            acc = acc - jnp.dot(tg[s], ys[...], preferred_element_type=jnp.float32)
            acc = acc.astype(jnp.bfloat16)
            for a, i in enumerate(pair):
                out_ref[s, :, columns(i)] = acc[:, a * 128 : (a + 1) * 128]

    def steps(step, lo, hi):
        lax.fori_loop(lo, hi, step, 0)

    tiles_near()
    loads[0].wait()
    for u in range(SUB):
        wr[0, u] = pick(at(8), u)
        wl[0, u] = pick(at(-7), u)
        rs_right(0, u).start()
        rs_left(0, u).start()
    own.start(0, 0)
    tiles_far()
    steps(rs_step, 1, 3)
    own.wait(0, 0)
    own.start(0, 1)
    tiles_back()
    steps(rs_step, 3, 4)
    own.wait(0, 1)
    own.start(1, 0)
    steps(rs_step, 4, 5)
    tiles_all()
    steps(rs_step, 5, 6)
    own.wait(1, 0)
    own.start(1, 1)
    steps(rs_step, 6, 7)
    tiles_in()
    panel.start(0, 0)
    steps(rs_step, 7, 8)
    for u in range(SUB):
        rs_right(RSR - 1, u).wait_recv()
        rs_left(RSL - 1, u).wait_recv()
        r[z, u] = pick(z, u) + wr[RSR, u] + wl[RSL, u]
        ag_right(0, u).start()
        ag_left(0, u).start()
    panel.wait(0, 0)
    panel.start(0, 1)
    own.wait(1, 1)
    own.sibling(c).start()
    steps(ag_step, 1, 2)
    panel.wait(0, 1)
    panel.start(1, 0)
    panel.sibling_piece(0, c, "start")
    steps(ag_step, 2, 3)
    own.sibling(1 - c).wait_recv()
    lax.fori_loop(0, 2, own_products, 0)
    steps(ag_step, 3, 4)
    panel.wait(1, 0)
    panel.start(1, 1)
    panel.sibling_piece(1, c, "start")
    panel.sibling_piece(3, c, "start")
    lax.fori_loop(2, 4, own_products, 0)
    steps(ag_step, 4, 5)
    lax.fori_loop(4, 6, own_products, 0)
    steps(ag_step, 5, 6)
    panel.wait(1, 1)
    panel.sibling_piece(2, c, "start")
    lax.fori_loop(6, 8, own_products, 0)
    steps(ag_step, 6, 7)
    for d in range(4):
        panel.sibling_piece(d, 1 - c, "wait_recv")
    loads[3].wait()
    panel_products()
    steps(ag_step, 7, 8)
    solve(0)
    update(0)
    for u in range(SUB):
        ag_right_in(RSR - 1, u).wait_recv()
        ag_left_in(RSL - 1, u).wait_recv()
    solve(1)
    update(1)

    def rs_done(t, _):
        for u in range(SUB):
            rs_right(t, u).wait_send()
            ag_right(t, u).wait_send()

            @pl.when(t < RSL)
            def _():
                rs_left(t, u).wait_send()
                ag_left(t, u).wait_send()
        return 0

    lax.fori_loop(0, RSR, rs_done, 0)
    tiles_done()
    own.wait_sends()
    panel.wait_sends()


def finish_kernel(psv_in, out_in, psv_ref, out_ref):
    psv_ref[...] = psv_in[...]
    out_ref[...] = out_in[...]


def local(right_side, diag_inverse, factor_u, factor_v, tile_rank, block_order):
    vmem = pl.BlockSpec(memory_space=pltpu.VMEM)
    smem = pl.BlockSpec(memory_space=pltpu.SMEM)
    anywhere = pl.BlockSpec(memory_space=pl.ANY)
    bf16 = jnp.bfloat16
    dma = pltpu.SemaphoreType.DMA
    results = (
        jax.ShapeDtypeStruct((4, 32, 512), bf16),
        jax.ShapeDtypeStruct((2, 512, 512), bf16),
    )
    solved = pl.pallas_call(
        kernel,
        out_shape=results,
        in_specs=[smem, smem] + [anywhere] * 4,
        out_specs=(vmem, vmem),
        scratch_shapes=[
            pltpu.VMEM((2, 512, 512), bf16),
            pltpu.VMEM((4, 512, 512), bf16),
            pltpu.VMEM((2, 4, 16, 384), bf16),
            pltpu.VMEM((2, 4, 16, 384), bf16),
            pltpu.VMEM((RSR + 1, 4, 128, 128), bf16),
            pltpu.VMEM((RSL + 1, 4, 128, 128), bf16),
            pltpu.VMEM((Z, 4, 128, 128), bf16),
            pltpu.VMEM((16, 4, 4, 2, 16, 384), bf16),
            pltpu.VMEM((12, 4, 4, 2, 16, 384), bf16),
            pltpu.VMEM((12, 16, 384), bf16),
            pltpu.VMEM((4, 3, 16, 384), bf16),
            pltpu.VMEM((3, 16, 384), bf16),
            pltpu.VMEM((4, 16, 384), bf16),
            pltpu.VMEM((2, 512, 2048), bf16),
            pltpu.VMEM((3, 512, 1536), bf16),
            pltpu.VMEM((2048, 256), bf16),
            dma((4,)),
            dma((RSR, SUB)), dma((RSR, SUB)), dma((RSL, SUB)), dma((RSL, SUB)),
            dma((RSR, SUB)), dma((RSR, SUB)), dma((RSL, SUB)), dma((RSL, SUB)),
            dma((4,)), dma((4,)), dma((4,)), dma((4,)), dma((4,)), dma((4,)), dma((4,)), dma((4,)),
            dma((17,)), dma((17,)), dma((24,)), dma((24,)),
        ],
        compiler_params=pltpu.CompilerParams(
            collective_id=0, has_side_effects=True, vmem_limit_bytes=56 * 2**20
        ),
        cost_estimate=pl.CostEstimate(flops=7_000_000_000, bytes_accessed=8_000_000, transcendentals=0),
    )(block_order, tile_rank, right_side, diag_inverse, factor_u, factor_v)
    return pl.pallas_call(finish_kernel, out_shape=results)(*solved)


def solution(mesh):
    placed = (
        P("rows", None, "src"),
        P(),
        P("rows", None, "src", None),
        P("rows", None, "src", None),
        P("rows", None),
        P(),
    )
    return jax.shard_map(
        local,
        mesh=mesh,
        in_specs=placed,
        out_specs=(P(None, "rows", "src"), P("rows", None, "src")),
        check_vma=False,
    )
```
